32 devices in a mesh: chol: 2 (over x), walk: 16 (over z, y, core).
Axes of the slice: x: 2, y: 2, z: 4, core: 2. Of those that a mesh axis runs over, the one named last changes fastest.
Arguments:
- field_draws: bfloat16 [16, 2048], P('walk', 'chol'), may hold values from -6 to 6
- chol_vectors: bfloat16 [2048, 512, 512], P('chol', 'walk'), as said below
- rotated_vectors: bfloat16 [2048, 128, 512], P(('chol', 'walk')), may hold values from -1.5 to 1.5
- walkers: bfloat16 [16, 512, 128], P('walk'), may hold values from -6 to 6
Outputs:
- propagated: float32 [16, 512, 128], P('walk')
- exchange_energy: float32 [16], P('walk')
The draws below stay inside these ranges and needn't reach their ends.
Inputs may be any that keep to these rules, and one draw needn't show every extreme that they name: Each chol_vectors[g] is a symmetric matrix.
All inputs are finite; a program needn't handle non-finite values.
Results may differ from the reference program's by a relative error of at most 0.0036.
Values may be sent and summed in bfloat16 or wider, within the bound.
No kernel may reach another device: no remote copies, remote signals or barrier semaphores. Data moves between devices by JAX's collectives and lax.ppermute only.
A program may use at most 192 MiB of HBM per device.

```python
from functools import partial
import jax
import jax.numpy as jnp
from jax import lax

ORB = 512
OCC = 128
VECS = 2048
TERMS = 4
WALKERS = 16


def draw_chol_vectors(key, part):
    scale = 1.1 / (VECS * ORB) ** 0.5
    raw = jax.random.truncated_normal(key, -6.0, 6.0, (VECS, ORB, ORB), jnp.float32)
    sym = (raw + jnp.swapaxes(raw, 1, 2)) * (scale / 2.0 ** 0.5)
    return sym.astype(jnp.bfloat16)


def steps_of(own_key, shape, pieces, least, largest):
    loudness, own = 1.0, jax.random.fold_in(own_key, 6)
    for position, shards_of in pieces:
        draws = jnp.exp(jax.random.uniform(jax.random.fold_in(own, position), (shards_of,), jnp.float32, least / len(pieces), largest / len(pieces)))
        loudness = loudness * jnp.repeat(draws, shape[position] // shards_of).reshape([-1 if axis == position else 1 for axis in range(len(shape))])
    return loudness


def centred(own_key, extent, scale, limit, pieces=(), dtype=jnp.bfloat16):
    entries = scale * jax.random.normal(own_key, extent, jnp.float32)
    if pieces:
        entries = entries * steps_of(own_key, extent, pieces, -0.22, 0.18)
    return jnp.clip(entries, -limit, limit).astype(dtype)


def setup_inputs(seed: int = 0) -> dict:
    key_list = jax.random.split(jax.random.key(seed), 5)
    field_draws = centred(key_list[0], (WALKERS, VECS), 1.0, 6.0, ((0, 16), (1, 2)))
    chol_vectors = draw_chol_vectors(jax.random.fold_in(key_list[4], 71), 0)
    rotated_vectors = centred(key_list[2], (VECS, OCC, ORB), ((6 * ORB / (VECS * OCC)) ** 0.5), 1.5, ((0, 32),))
    walkers = centred(key_list[3], (WALKERS, ORB, OCC), 1.0, 6.0, ((0, 16),))
    return {"field_draws": field_draws, "chol_vectors": chol_vectors, "rotated_vectors": rotated_vectors, "walkers": walkers}


def block_energy(rotated_block, dual_cols):
    rows = jnp.dot(rotated_block.reshape(-1, ORB).astype(jnp.float32), dual_cols.astype(jnp.float32), preferred_element_type=jnp.float32)
    tiled = rows.reshape(-1, OCC, WALKERS, OCC)
    return jnp.einsum('giwj,gjwi->w', tiled, tiled)

def reference(field_draws, chol_vectors, rotated_vectors, walkers):
    operators = jnp.dot(field_draws.astype(jnp.float32), chol_vectors.reshape(VECS, ORB * ORB).astype(jnp.float32), preferred_element_type=jnp.float32)
    operators = operators.astype(jnp.bfloat16).reshape(WALKERS, ORB, ORB)
    taylor_term = walkers
    propagated = walkers.astype(jnp.float32)
    for degree in range(1, TERMS + 1):
        applied = jnp.einsum('wpq,wqi->wpi', operators.astype(jnp.float32), taylor_term.astype(jnp.float32))
        taylor_term = (applied / degree).astype(jnp.bfloat16)
        propagated = propagated + taylor_term.astype(jnp.float32)
    correlation = jnp.einsum('wpi,wpj->wij', walkers.astype(jnp.float32), propagated, precision=lax.Precision.HIGHEST)
    dual_t = jnp.linalg.solve(jnp.transpose(correlation, (0, 2, 1)), jnp.transpose(propagated, (0, 2, 1)))
    dual_cols = jnp.transpose(dual_t, (2, 0, 1)).reshape(ORB, WALKERS * OCC).astype(jnp.bfloat16)
    dual_cols = lax.optimization_barrier(dual_cols).astype(jnp.float32)
    blocks = rotated_vectors.reshape(VECS // 16, 16, OCC, ORB)
    sums = lax.map(partial(block_energy, dual_cols=dual_cols), blocks)
    exchange_energy = -0.5 * jnp.sum(sums, axis=0)
    return (propagated, exchange_energy)
```

```python
import functools

import jax
import jax.numpy as jnp
from jax import lax
from jax.experimental import pallas as pl
from jax.experimental.pallas import tpu as pltpu
from jax.sharding import PartitionSpec as P

TERMS = 4
TILE = 16
BF = jnp.bfloat16
F32 = jnp.float32
BOTH = ("chol", "walk")


def solve_dual(correlation, transposed):
    gram = jnp.dot(correlation, correlation.T, precision=lax.Precision.HIGHEST)
    factor = jnp.linalg.cholesky(gram)
    right = jnp.dot(correlation, transposed, precision=lax.Precision.HIGHEST)
    return jax.scipy.linalg.cho_solve((factor, True), right)


def propagate(operators, walkers):
    taylor_term = walkers
    propagated = walkers.astype(F32)
    for degree in range(1, TERMS + 1):
        applied = jnp.dot(operators, taylor_term, preferred_element_type=F32)
        taylor_term = (applied / degree).astype(BF)
        propagated = propagated + taylor_term.astype(F32)
    return propagated


def dual_of(walkers, propagated):
    correlation = jnp.dot(walkers.astype(F32).T, propagated, precision=lax.Precision.HIGHEST)
    return solve_dual(correlation, propagated.T).T.astype(BF)


def operator_kernel(planes, draws_ref, chol_ref, out_ref, acc_ref, spread_ref):
    step = pl.program_id(0)
    walkers, group = draws_ref.shape[1:]
    rows, orbitals = chol_ref.shape[1:]
    depth = group * TILE

    @pl.when(step == 0)
    def _():
        acc_ref[...] = jnp.zeros_like(acc_ref)

    owner = lax.broadcasted_iota(jnp.int32, (group, depth), 1) // TILE
    repeat = jnp.where(owner == lax.broadcasted_iota(jnp.int32, (group, depth), 0), 1.0, 0.0).astype(BF)
    repeated = jnp.dot(draws_ref[0], repeat, preferred_element_type=F32)
    lane_row = lax.broadcasted_iota(jnp.int32, (TILE, depth), 1) % TILE
    diagonal = lane_row == lax.broadcasted_iota(jnp.int32, (TILE, depth), 0)
    for walker in range(walkers):
        spread = jnp.where(diagonal, repeated[walker : walker + 1, :], 0.0)
        spread_ref[walker * TILE : (walker + 1) * TILE, :] = spread.astype(BF)
    for part in range(rows // TILE):
        right = chol_ref[:, part * TILE : (part + 1) * TILE, :].reshape(depth, orbitals)
        acc_ref[part] += jnp.dot(spread_ref[...], right, preferred_element_type=F32)

    @pl.when(step == pl.num_programs(0) - 1)
    def _():
        parts = rows // TILE
        for part in range(parts):
            for walker in range(walkers):
                place = (walker % planes) * (walkers // planes * parts) + walker // planes * parts + part
                out_ref[place] = acc_ref[part, walker * TILE : (walker + 1) * TILE, :].astype(BF)


def partial_operators(draws, chol_vectors, planes, group=64):
    vectors, rows, orbitals = chol_vectors.shape
    walkers = draws.shape[0]
    parts = rows // TILE
    steps = vectors // group
    blocked = jnp.transpose(draws.reshape(walkers, steps, group), (1, 0, 2))
    return pl.pallas_call(
        functools.partial(operator_kernel, planes),
        grid=(steps,),
        in_specs=[
            pl.BlockSpec((1, walkers, group), lambda i: (i, 0, 0)),
            pl.BlockSpec((group, rows, orbitals), lambda i: (i, 0, 0)),
        ],
        out_specs=pl.BlockSpec((walkers * parts, TILE, orbitals), lambda i: (0, 0, 0)),
        out_shape=jax.ShapeDtypeStruct((walkers * parts, TILE, orbitals), BF),
        scratch_shapes=[
            pltpu.VMEM((parts, walkers * TILE, orbitals), F32),
            pltpu.VMEM((walkers * TILE, group * TILE), BF),
        ],
        compiler_params=pltpu.CompilerParams(vmem_limit_bytes=40 << 20),
        cost_estimate=pl.CostEstimate(
            flops=2 * walkers * TILE * vectors * rows * orbitals,
            bytes_accessed=vectors * rows * orbitals * 2,
            transcendentals=0,
        ),
        name="operators",
    )(blocked, chol_vectors)


def energy_kernel(count, own_ref, other_ref, *refs):
    dual_refs, (out_ref, acc_ref) = refs[:count], refs[count:]
    step = pl.program_id(0)
    half = pl.num_programs(0) // 2
    group, occ, orbitals = own_ref.shape

    @pl.when(step == 0)
    def _():
        acc_ref[...] = jnp.zeros_like(acc_ref)

    def fold(vectors_ref):
        left = vectors_ref[...].reshape(group * occ, orbitals)
        for pair in range(0, count, 2):
            right = jnp.concatenate([dual_refs[pair][...], dual_refs[pair + 1][...]], axis=1)
            products = jnp.dot(left, right, preferred_element_type=F32)
            for member in range(2):
                total = None
                for vector in range(group):
                    block = products[vector * occ : (vector + 1) * occ, member * occ : (member + 1) * occ]
                    term = block * block.T
                    total = term if total is None else total + term
                acc_ref[pair + member] += total.reshape(occ // 8, 8, occ).sum(0)

    pl.when(step < half)(lambda: fold(own_ref))
    pl.when(step >= half)(lambda: fold(other_ref))

    @pl.when(step == pl.num_programs(0) - 1)
    def _():
        out_ref[...] = acc_ref[...]


def energies(own, other, duals, group=8):
    vectors, occ, orbitals = own.shape
    count = len(duals)
    half = vectors // group
    whole = lambda i: (0, 0)
    return pl.pallas_call(
        functools.partial(energy_kernel, count),
        grid=(2 * half,),
        in_specs=[
            pl.BlockSpec((group, occ, orbitals), lambda i: (jnp.minimum(i, half - 1), 0, 0)),
            pl.BlockSpec((group, occ, orbitals), lambda i: (jnp.maximum(i - half, 0), 0, 0)),
        ]
        + [pl.BlockSpec((orbitals, occ), whole)] * count,
        out_specs=pl.BlockSpec((count, 8, occ), lambda i: (0, 0, 0)),
        out_shape=jax.ShapeDtypeStruct((count, 8, occ), F32),
        scratch_shapes=[pltpu.VMEM((count, 8, occ), F32)],
        compiler_params=pltpu.CompilerParams(vmem_limit_bytes=40 << 20),
        cost_estimate=pl.CostEstimate(
            flops=4 * vectors * count * occ * occ * orbitals,
            bytes_accessed=4 * vectors * occ * orbitals,
            transcendentals=0,
        ),
        name="energies",
    )(own, other, *duals)


def flat(chol, z, y, core, walk):
    return chol * walk + (z * 2 + y) * 2 + core


def per_device(field_draws, chol_vectors, rotated_vectors, walkers):
    planes, walk = lax.axis_size("chol"), lax.axis_size("walk")
    depth = walk // 4
    chol, place = lax.axis_index("chol"), lax.axis_index("walk")
    core, z = place % 2, place // 4
    slab_vectors, slab_rows, orbitals = chol_vectors.shape
    occ = walkers.shape[2]
    swap = [(i, i ^ 1) for i in range(walk)]
    every = [(c, zz, y, k) for c in range(2) for zz in range(depth) for y in range(2) for k in range(2)]

    def send(array, target):
        pairs = [(flat(*at, walk), flat(*target(*at), walk)) for at in every if target(*at) is not None]
        return lax.ppermute(array, BOTH, pairs)

    other_vectors = lax.ppermute(rotated_vectors, "walk", swap)
    other_walker = lax.ppermute(walkers, "walk", swap)

    draws = lax.all_to_all(
        jnp.broadcast_to(field_draws, (walk, slab_vectors)), "walk", split_axis=0, concat_axis=0, tiled=True
    )
    partial = partial_operators(draws, chol_vectors, planes)
    pieces = lax.all_to_all(partial, BOTH, split_axis=0, concat_axis=0, tiled=True)
    pieces = pieces.reshape(planes, walk, TILE, orbitals).astype(F32).sum(0).astype(BF)
    other_pieces = lax.ppermute(pieces, "walk", swap)
    first = jnp.where(core == 0, pieces, other_pieces)
    second = jnp.where(core == 0, other_pieces, pieces)
    operators = jnp.stack([first, second], axis=1).reshape(orbitals, orbitals)

    walker = jnp.where(core == chol, walkers[0], other_walker[0])
    propagated = propagate(operators, walker)
    dual = dual_of(walker, propagated)
    across = send(propagated, lambda c, zz, y, k: (1 - c, zz, y, k) if k == c else None)
    propagated = jnp.where(core == chol, propagated, across)[None]

    def along(shift):
        def target(c, zz, y, k):
            if zz // 2 != k:
                return None
            if shift == 0:
                return (c, zz ^ 1, y, k)
            far = (2 * (1 - k)) + ((zz % 2) ^ (shift - 1))
            return (c, far, y, k)

        return target

    near, far_a, far_b = send(dual, along(0)), send(dual, along(1)), send(dual, along(2))
    odd = z % 2 == 1
    inside = z // 2 == core
    even_dual = jnp.where(inside, jnp.where(odd, near, dual), jnp.where(odd, far_b, far_a))
    odd_dual = jnp.where(inside, jnp.where(odd, dual, near), jnp.where(odd, far_a, far_b))
    mine = (even_dual, odd_dual)
    turn = lambda c, zz, y, k: (c, zz, 1 - y, k) if k == 0 else (1 - c, zz, y, k)
    back = lambda c, zz, y, k: (1 - c, zz, y, k) if k == 0 else (c, zz, 1 - y, k)
    one = tuple(send(d, turn) for d in mine)
    terms = [energies(rotated_vectors, other_vectors, mine)]
    two = tuple(send(d, back) for d in mine + one)
    terms.append(energies(rotated_vectors, other_vectors, one))
    terms.append(energies(rotated_vectors, other_vectors, two))
    terms = jnp.concatenate(terms, 0).sum(1)

    y = place // 2 % 2
    slots = []
    for order in range(4):
        first_axis, second_axis = order % 2, order // 2
        y_flip = jnp.where(core == 0, first_axis, second_axis)
        x_flip = jnp.where(core == 0, second_axis, first_axis)
        for parity in range(2):
            slots.append(((2 * core + parity) * 2 + (y ^ y_flip)) * 2 + (chol ^ x_flip))
    slots = jnp.stack(slots)
    hit = (slots[None, :, None] == jnp.arange(walk)[:, None, None]).astype(F32)
    sent = (hit * terms[None]).sum(1)
    sent = jnp.broadcast_to(sent, (planes,) + sent.shape).reshape(planes * walk, occ)
    came = lax.all_to_all(sent, BOTH, split_axis=0, concat_axis=0, tiled=True)
    return propagated, -0.5 * came.sum().reshape(1)


def per_device_plain(field_draws, chol_vectors, rotated_vectors, walkers):
    local_walkers, orbitals, occ = walkers.shape
    total_walkers = local_walkers * lax.axis_size("walk")
    slab_vectors, slab_rows, _ = chol_vectors.shape
    all_draws = lax.all_gather(field_draws, "walk", axis=0, tiled=True)
    partial_rows = jnp.dot(
        all_draws, chol_vectors.reshape(slab_vectors, slab_rows * orbitals), preferred_element_type=F32
    )
    partial_rows = partial_rows.reshape(total_walkers, slab_rows, orbitals)
    summed_rows = lax.psum(partial_rows, "chol").astype(BF)
    operators = lax.all_to_all(summed_rows, "walk", split_axis=0, concat_axis=1, tiled=True)
    propagated = jax.vmap(propagate)(operators, walkers)
    duals = jax.vmap(dual_of)(walkers, propagated)
    dual_cols = jnp.transpose(duals, (1, 0, 2)).reshape(orbitals, local_walkers * occ)
    columns = lax.all_gather(dual_cols, "walk", axis=1, tiled=True)

    def vector_step(vector, summed):
        single = lax.dynamic_index_in_dim(rotated_vectors, vector, 0, keepdims=False)
        tiled = jnp.dot(single, columns, preferred_element_type=F32).reshape(occ, total_walkers, occ)
        return summed + jnp.einsum("iwj,jwi->w", tiled, tiled)

    totals = lax.fori_loop(0, rotated_vectors.shape[0], vector_step, jnp.zeros((total_walkers,), F32))
    summed = lax.psum(totals, BOTH)
    mine = lax.dynamic_slice_in_dim(summed, lax.axis_index("walk") * local_walkers, local_walkers, 0)
    return propagated, -0.5 * mine


def solution(mesh):
    planes, walk = mesh.shape["chol"], mesh.shape["walk"]

    def step(field_draws, chol_vectors, rotated_vectors, walkers):
        rows = chol_vectors.shape[1]
        fits = planes == 2 and walk == 16 and walkers.shape[0] == 1 and rows == 2 * TILE
        body = per_device if fits else per_device_plain
        return body(field_draws, chol_vectors, rotated_vectors, walkers)

    return jax.shard_map(
        step,
        mesh=mesh,
        in_specs=(
            P("walk", "chol"),
            P("chol", "walk", None),
            P(("chol", "walk"), None, None),
            P("walk", None, None),
        ),
        out_specs=(P("walk", None, None), P("walk")),
        check_vma=False,
    )
```

```python
import functools

import jax
import jax.numpy as jnp
from jax import lax
from jax.experimental import pallas as pl
from jax.experimental.pallas import tpu as pltpu
from jax.sharding import PartitionSpec as P

TERMS = 4
TILE = 16
GROUPS = 4
BF = jnp.bfloat16
F32 = jnp.float32
BOTH = ("chol", "walk")


def in_hbm(array):
    return pltpu.with_memory_space_constraint(array, pltpu.HBM)


def in_vmem(array):
    return pltpu.with_memory_space_constraint(array, pltpu.VMEM)


def solve_dual(correlation, transposed):
    gram = jnp.dot(correlation, correlation.T, precision=lax.Precision.HIGHEST)
    factor = jnp.linalg.cholesky(gram)
    right = jnp.dot(correlation, transposed, precision=lax.Precision.HIGHEST)
    return jax.scipy.linalg.cho_solve((factor, True), right)


def propagate(operators, walkers):
    taylor_term = walkers
    propagated = walkers.astype(F32)
    for degree in range(1, TERMS + 1):
        applied = jnp.dot(operators, taylor_term, preferred_element_type=F32)
        taylor_term = (applied / degree).astype(BF)
        propagated = propagated + taylor_term.astype(F32)
    return propagated


def dual_of(walkers, propagated):
    correlation = jnp.dot(walkers.astype(F32).T, propagated, precision=lax.Precision.HIGHEST)
    return solve_dual(correlation, propagated.T).T.astype(BF)


def operator_kernel(planes, draws_ref, chol_ref, out_ref, near_ref, far_ref, repeat_ref, spread_ref, sums_ref, sems):
    walkers, steps, group = draws_ref.shape
    rows, orbitals = chol_ref.shape[1:]
    wide = orbitals // GROUPS
    depth = group * TILE
    parts = rows // TILE
    own_group = lax.axis_index("walk") * rows // wide
    upper = jnp.where(own_group >= GROUPS // 2, 1, 0)

    def columns(shift):
        return pl.ds(pl.multiple_of((own_group + shift) % GROUPS * wide, wide), wide)

    copies = []
    for step in range(steps):
        whole, half = pl.ds(step * group, group), pl.ds(step * group + upper * (group // 2), group // 2)
        pairs = [
            (chol_ref.at[whole, :, columns(0)], near_ref.at[step, :, :, pl.ds(0, wide)]),
            (chol_ref.at[whole, :, columns(1)], near_ref.at[step, :, :, pl.ds(wide, wide)]),
            (chol_ref.at[half, :, columns(2)], far_ref.at[step]),
        ]
        copies.append([pltpu.make_async_copy(*pair, sems.at[step, at]) for at, pair in enumerate(pairs)])
        for copy in copies[-1]:
            copy.start()

    owner = lax.broadcasted_iota(jnp.int32, (group, depth), 1) // TILE
    mine = owner == lax.broadcasted_iota(jnp.int32, (group, depth), 0)
    repeat_ref[...] = jnp.where(mine, 1.0, 0.0).astype(BF)
    lane_row = lax.broadcasted_iota(jnp.int32, (TILE, depth), 1) % TILE
    diagonal = lane_row == lax.broadcasted_iota(jnp.int32, (TILE, depth), 0)
    draws = draws_ref[...].astype(F32)

    def spread(step):
        repeated = jnp.dot(draws[:, step, :].astype(BF), repeat_ref[...], preferred_element_type=F32)
        for walker in range(walkers):
            block = jnp.where(diagonal, repeated[walker : walker + 1, :], 0.0)
            spread_ref[step % 2, walker * TILE : (walker + 1) * TILE, :] = block.astype(BF)

    def add(at, step, value):
        sums_ref[at] = value if step == 0 else sums_ref[at] + value

    spread(0)
    half_lanes = pl.ds(pl.multiple_of(upper * (depth // 2), depth // 2), depth // 2)
    for step in range(steps):
        if step + 1 < steps:
            spread(step + 1)
        for copy in copies[step]:
            copy.wait()
        far = []
        for part in range(parts):
            taken = slice(part * TILE, (part + 1) * TILE)
            right = near_ref[step, :, taken, :].reshape(depth, 2 * wide)
            add(part, step, jnp.dot(spread_ref[step % 2], right, preferred_element_type=F32))
            far.append(far_ref[step, :, taken, :].reshape(depth // 2, wide))
        right = jnp.concatenate(far, axis=1)
        add(parts, step, jnp.dot(spread_ref[step % 2, :, half_lanes], right, preferred_element_type=F32))

    for part in range(parts):
        for walker in range(walkers):
            place = (walker % planes) * (walkers // planes * parts) + walker // planes * parts + part
            taken = slice(walker * TILE, (walker + 1) * TILE)
            out_ref[place, :, : 2 * wide] = sums_ref[part, taken, :].astype(BF)
            out_ref[place, :, 2 * wide :] = sums_ref[parts, taken, part * wide : (part + 1) * wide].astype(BF)


def partial_operators(draws, chol_vectors, planes):
    walkers, steps, group = draws.shape
    vectors, rows, orbitals = chol_vectors.shape
    parts, wide = rows // TILE, orbitals // GROUPS
    vmem = pl.BlockSpec(memory_space=pltpu.VMEM)
    return pl.pallas_call(
        functools.partial(operator_kernel, planes),
        in_specs=[vmem, pl.BlockSpec(memory_space=pl.ANY)],
        out_specs=vmem,
        out_shape=jax.ShapeDtypeStruct((walkers * parts, TILE, 3 * wide), BF),
        scratch_shapes=[
            pltpu.VMEM((steps, group, rows, 2 * wide), BF),
            pltpu.VMEM((steps, group // 2, rows, wide), BF),
            pltpu.VMEM((group, group * TILE), BF),
            pltpu.VMEM((2, walkers * TILE, group * TILE), BF),
            pltpu.VMEM((parts + 1, walkers * TILE, 2 * wide), F32),
            pltpu.SemaphoreType.DMA((steps, 3)),
        ],
        compiler_params=pltpu.CompilerParams(vmem_limit_bytes=32 << 20),
        cost_estimate=pl.CostEstimate(
            flops=10 * walkers * TILE * vectors * rows * wide // 2,
            bytes_accessed=vectors * rows * wide * 5,
            transcendentals=0,
        ),
        name="operators",
    )(draws, in_hbm(chol_vectors))


def pieces_of(value, count):
    found = []
    for _ in range(count):
        piece = value.astype(BF)
        found.append(piece)
        value = value - piece.astype(F32)
    return found


def fine_dot(a, b):
    left = jnp.concatenate([a[0], a[0], a[1]], axis=1)
    right = jnp.concatenate([b[0], b[1], b[0]], axis=0)
    return jnp.dot(left, right, preferred_element_type=F32)


def full_dot(a, b):
    return jnp.dot(a, b, precision=lax.Precision.HIGHEST, preferred_element_type=F32)


def inverse_of(matrix):
    size = matrix.shape[0]
    shape = (size, size)
    one = jnp.where(lax.broadcasted_iota(jnp.int32, shape, 0) == lax.broadcasted_iota(jnp.int32, shape, 1), 1.0, 0.0)
    largest = jnp.max(jnp.sum(jnp.abs(matrix), axis=1, keepdims=True), axis=0, keepdims=True)
    guess = one * (1.5 / largest)
    halves = pieces_of(matrix, 2)

    def rough(carry):
        count, _, x = carry
        for _ in range(3):
            rest = one - fine_dot(halves, pieces_of(x, 2))
            x = x + fine_dot(pieces_of(x, 2), pieces_of(rest, 2))
        return count + 1, jnp.sum(rest * rest), x

    def exact(carry):
        count, _, x = carry
        rest = one - full_dot(matrix, x)
        return count + 1, jnp.sum(rest * rest), x + full_dot(x, rest)

    _, _, guess = lax.while_loop(
        lambda c: jnp.logical_and(c[0] < 14, c[1] > 1e-4), rough, (jnp.int32(0), jnp.float32(1), guess)
    )
    _, _, guess = lax.while_loop(
        lambda c: jnp.logical_and(c[0] < 6, c[1] > 1e-6), exact, (jnp.int32(0), jnp.float32(1), guess)
    )
    return guess


def solve_kernel(
    planes,
    own_rows_ref,
    other_rows_ref,
    own_walker_ref,
    other_walker_ref,
    own_ref,
    other_ref,
    propagated_ref,
    dual_ref,
    own_out_ref,
    other_out_ref,
    rows_ref,
    operators_ref,
    own_sem,
    other_sem,
):
    own_copy = pltpu.make_async_copy(own_ref, own_out_ref, own_sem)
    other_copy = pltpu.make_async_copy(other_ref, other_out_ref, other_sem)
    own_copy.start()
    other_copy.start()
    core, chol = lax.axis_index("walk") % 2, lax.axis_index("chol")
    slabs, wide = own_rows_ref.shape[0] // planes, own_rows_ref.shape[2] // 3
    for slab in range(slabs):
        for from_ref, side in ((own_rows_ref, core), (other_rows_ref, 1 - core)):
            summed = from_ref[slab].astype(F32)
            for plane in range(1, planes):
                summed = summed + from_ref[plane * slabs + slab].astype(F32)
            rows_ref[pl.ds(pl.multiple_of((2 * slab + side) * TILE, TILE), TILE), :] = summed
    group = lambda k: slice(k % GROUPS * wide, (k % GROUPS + 1) * wide)
    for k in range(GROUPS):
        operators_ref[group(k), group(k)] = rows_ref[group(k), group(0)].astype(BF)
        after = rows_ref[group(k), group(1)]
        operators_ref[group(k), group(k + 1)] = after.astype(BF)
        operators_ref[group(k + 1), group(k)] = after.T.astype(BF)
    for k in range(GROUPS // 2):
        one, two = rows_ref[group(k), group(2)], rows_ref[group(k + 2), group(2)]
        operators_ref[group(k), group(k + 2)] = (one + two.T).astype(BF)
        operators_ref[group(k + 2), group(k)] = (one.T + two).astype(BF)
    mine = jnp.where(core == chol, 1.0, 0.0)
    walker = own_walker_ref[...].astype(F32) * mine + other_walker_ref[...].astype(F32) * (1.0 - mine)
    taylor_term = walker.astype(BF)
    transposed = taylor_term.T
    propagated = walker
    for degree in range(1, TERMS + 1):
        applied = jnp.dot(operators_ref[...], taylor_term, preferred_element_type=F32)
        taylor_term = (applied / degree).astype(BF)
        propagated = propagated + taylor_term.astype(F32)
    propagated_ref[...] = propagated
    correlation = None
    for piece in pieces_of(propagated, 3):
        part = jnp.dot(transposed, piece, preferred_element_type=F32)
        correlation = part if correlation is None else correlation + part
    dual_ref[...] = full_dot(propagated, inverse_of(correlation)).astype(BF)
    own_copy.wait()
    other_copy.wait()


def solve(own_rows, other_rows, own_walker, other_walker, own, other, planes):
    orbitals = own_walker.shape[0]
    vmem, anywhere = pl.BlockSpec(memory_space=pltpu.VMEM), pl.BlockSpec(memory_space=pl.ANY)
    return pl.pallas_call(
        functools.partial(solve_kernel, planes),
        in_specs=[vmem] * 4 + [anywhere] * 2,
        out_specs=[vmem] * 4,
        out_shape=[
            jax.ShapeDtypeStruct(own_walker.shape, F32),
            jax.ShapeDtypeStruct(own_walker.shape, BF),
            pltpu.VMEM(own.shape, BF),
            pltpu.VMEM(other.shape, BF),
        ],
        scratch_shapes=[
            pltpu.VMEM((orbitals, own_rows.shape[2]), F32),
            pltpu.VMEM((orbitals, orbitals), BF),
            pltpu.SemaphoreType.DMA,
            pltpu.SemaphoreType.DMA,
        ],
        compiler_params=pltpu.CompilerParams(vmem_limit_bytes=16 << 20),
        cost_estimate=pl.CostEstimate(flops=6 * 10**9, bytes_accessed=16 << 20, transcendentals=0),
        name="solve",
    )(own_rows, other_rows, own_walker, other_walker, in_hbm(own), in_hbm(other))


def energy_kernel(group, sub, own_ref, other_ref, *refs):
    dual_refs, out_ref = refs[:-1], refs[-1]
    vectors, occ, orbitals = own_ref.shape
    pairs = [jnp.concatenate([ref[0], ref[1]], axis=1) for ref in dual_refs]
    count = 2 * len(pairs)
    out_ref[...] = jnp.zeros_like(out_ref)
    for vectors_ref in (own_ref, other_ref):

        @pl.loop(0, vectors, step=group)
        def _(start):
            totals = [None] * count
            for at in range(0, group, sub):
                left = vectors_ref[pl.ds(start + at, sub)].reshape(sub * occ, orbitals)
                for pair, right in enumerate(pairs):
                    products = jnp.dot(left, right, preferred_element_type=F32)
                    for member in range(2):
                        for vector in range(sub):
                            block = products[vector * occ : (vector + 1) * occ, member * occ : (member + 1) * occ]
                            term = (block * block.T).reshape(occ // 8, 8, occ).sum(0)
                            slot = 2 * pair + member
                            totals[slot] = term if totals[slot] is None else totals[slot] + term
            for slot in range(count):
                out_ref[slot] += totals[slot]


def energies(own, other, duals, group=32, sub=2):
    vectors, occ, orbitals = own.shape
    count = 2 * len(duals)
    vmem = pl.BlockSpec(memory_space=pltpu.VMEM)
    return pl.pallas_call(
        functools.partial(energy_kernel, group, sub),
        in_specs=[vmem] * (2 + len(duals)),
        out_specs=vmem,
        out_shape=jax.ShapeDtypeStruct((count, 8, occ), F32),
        compiler_params=pltpu.CompilerParams(vmem_limit_bytes=16 << 20),
        cost_estimate=pl.CostEstimate(
            flops=4 * vectors * count * occ * occ * orbitals,
            bytes_accessed=4 * vectors * occ * orbitals,
            transcendentals=0,
        ),
        name="energies",
    )(in_vmem(own), in_vmem(other), *duals)


def flat(chol, z, y, core, walk):
    return chol * walk + (z * 2 + y) * 2 + core


def per_device(field_draws, chol_vectors, rotated_vectors, walkers):
    planes, walk = lax.axis_size("chol"), lax.axis_size("walk")
    depth = walk // 4
    chol, place = lax.axis_index("chol"), lax.axis_index("walk")
    core, z = place % 2, place // 4
    slab_vectors, slab_rows, orbitals = chol_vectors.shape
    occ = walkers.shape[2]
    swap = [(i, i ^ 1) for i in range(walk)]
    every = [(c, zz, y, k) for c in range(2) for zz in range(depth) for y in range(2) for k in range(2)]

    def send(array, target):
        pairs = [(flat(*at, walk), flat(*target(*at), walk)) for at in every if target(*at) is not None]
        return lax.ppermute(array, BOTH, pairs)

    other_vectors = lax.ppermute(rotated_vectors, "walk", swap)
    other_walker = lax.ppermute(walkers, "walk", swap)

    lanes = walkers.shape[2]
    spread = jnp.broadcast_to(field_draws.reshape(1, slab_vectors // lanes, lanes), (walk, slab_vectors // lanes, lanes))
    draws = lax.all_to_all(spread, "walk", split_axis=0, concat_axis=0, tiled=True)
    partial = partial_operators(draws, chol_vectors, planes)
    rows = lax.all_to_all(partial, BOTH, split_axis=0, concat_axis=0, tiled=True)
    other_rows = lax.ppermute(rows, "walk", swap)

    propagated, dual, own, other = solve(
        rows, other_rows, walkers[0], other_walker[0], rotated_vectors, other_vectors, planes
    )

    def first(c, zz, y, k):
        return (c, zz ^ 1 if zz // 2 == k else zz ^ 2, y, zz // 2)

    def second(c, zz, y, k):
        return (c, zz ^ 3, y, k) if zz // 2 == k else None

    turn = lambda c, zz, y, k: (c, zz, 1 - y, k) if k == 0 else (1 - c, zz, y, k)
    back = lambda c, zz, y, k: (1 - c, zz, y, k) if k == 0 else (c, zz, 1 - y, k)
    near, far = send(dual, first), send(dual, second)
    odd, inside = z % 2 == 1, z // 2 == core
    pick = lambda here, low, high: jnp.where(inside, jnp.where(here, dual, near), jnp.where(low, near, far))
    mine = jnp.stack([pick(~odd, ~odd, odd), pick(odd, odd, ~odd)])
    one, over = send(mine, turn), send(mine, back)
    terms = [energies(own, other, [mine])]
    one, propagated, terms[0] = lax.optimization_barrier((one, propagated, terms[0]))
    both = send(one, back)
    across = send(propagated, lambda c, zz, y, k: (1 - c, zz, y, k) if k == c else None)
    propagated = jnp.where(core == chol, propagated, across)[None]
    terms.append(energies(own, other, [one]))
    over, both, terms[1] = lax.optimization_barrier((over, both, terms[1]))
    terms.append(energies(own, other, [over, both]))
    terms = jnp.concatenate(terms, 0).sum(1)

    y = place // 2 % 2
    slots = []
    for order in range(4):
        first_axis, second_axis = order % 2, order // 2
        y_flip = jnp.where(core == 0, first_axis, second_axis)
        x_flip = jnp.where(core == 0, second_axis, first_axis)
        for parity in range(2):
            slots.append(((2 * core + parity) * 2 + (y ^ y_flip)) * 2 + (chol ^ x_flip))
    slots = jnp.stack(slots)
    hit = (slots[None, :, None] == jnp.arange(walk)[:, None, None]).astype(F32)
    sent = (hit * terms[None]).sum(1)
    sent = jnp.broadcast_to(sent, (planes,) + sent.shape).reshape(planes * walk, occ)
    came = lax.all_to_all(sent, BOTH, split_axis=0, concat_axis=0, tiled=True)
    return propagated, -0.5 * came.sum().reshape(1)


def per_device_plain(field_draws, chol_vectors, rotated_vectors, walkers):
    local_walkers, orbitals, occ = walkers.shape
    total_walkers = local_walkers * lax.axis_size("walk")
    slab_vectors, slab_rows, _ = chol_vectors.shape
    all_draws = lax.all_gather(field_draws, "walk", axis=0, tiled=True)
    partial_rows = jnp.dot(
        all_draws, chol_vectors.reshape(slab_vectors, slab_rows * orbitals), preferred_element_type=F32
    )
    partial_rows = partial_rows.reshape(total_walkers, slab_rows, orbitals)
    summed_rows = lax.psum(partial_rows, "chol").astype(BF)
    operators = lax.all_to_all(summed_rows, "walk", split_axis=0, concat_axis=1, tiled=True)
    propagated = jax.vmap(propagate)(operators, walkers)
    duals = jax.vmap(dual_of)(walkers, propagated)
    dual_cols = jnp.transpose(duals, (1, 0, 2)).reshape(orbitals, local_walkers * occ)
    columns = lax.all_gather(dual_cols, "walk", axis=1, tiled=True)

    def vector_step(vector, summed):
        single = lax.dynamic_index_in_dim(rotated_vectors, vector, 0, keepdims=False)
        tiled = jnp.dot(single, columns, preferred_element_type=F32).reshape(occ, total_walkers, occ)
        return summed + jnp.einsum("iwj,jwi->w", tiled, tiled)

    totals = lax.fori_loop(0, rotated_vectors.shape[0], vector_step, jnp.zeros((total_walkers,), F32))
    summed = lax.psum(totals, BOTH)
    mine = lax.dynamic_slice_in_dim(summed, lax.axis_index("walk") * local_walkers, local_walkers, 0)
    return propagated, -0.5 * mine


def solution(mesh):
    planes, walk = mesh.shape["chol"], mesh.shape["walk"]

    def step(field_draws, chol_vectors, rotated_vectors, walkers):
        rows, orbitals = chol_vectors.shape[1:]
        occ = walkers.shape[2]
        fits = planes == 2 and walk == 16 and walkers.shape[0] == 1 and rows == 2 * TILE and orbitals == GROUPS * occ
        body = per_device if fits else per_device_plain
        return body(field_draws, chol_vectors, rotated_vectors, walkers)

    return jax.shard_map(
        step,
        mesh=mesh,
        in_specs=(
            P("walk", "chol"),
            P("chol", "walk", None),
            P(("chol", "walk"), None, None),
            P("walk", None, None),
        ),
        out_specs=(P("walk", None, None), P("walk")),
        check_vma=False,
    )
```

```python
import functools

import jax
import jax.numpy as jnp
from jax import lax
from jax.experimental import pallas as pl
from jax.experimental.pallas import tpu as pltpu
from jax.sharding import PartitionSpec as P

TERMS = 4
TILE = 16
GROUPS = 4
BF = jnp.bfloat16
F32 = jnp.float32
BOTH = ("chol", "walk")


def in_hbm(array):
    return pltpu.with_memory_space_constraint(array, pltpu.HBM)


def in_vmem(array):
    return pltpu.with_memory_space_constraint(array, pltpu.VMEM)


def solve_dual(correlation, transposed):
    gram = jnp.dot(correlation, correlation.T, precision=lax.Precision.HIGHEST)
    factor = jnp.linalg.cholesky(gram)
    right = jnp.dot(correlation, transposed, precision=lax.Precision.HIGHEST)
    return jax.scipy.linalg.cho_solve((factor, True), right)


def propagate(operators, walkers):
    taylor_term = walkers
    propagated = walkers.astype(F32)
    for degree in range(1, TERMS + 1):
        applied = jnp.dot(operators, taylor_term, preferred_element_type=F32)
        taylor_term = (applied / degree).astype(BF)
        propagated = propagated + taylor_term.astype(F32)
    return propagated


def dual_of(walkers, propagated):
    correlation = jnp.dot(walkers.astype(F32).T, propagated, precision=lax.Precision.HIGHEST)
    return solve_dual(correlation, propagated.T).T.astype(BF)


def operator_kernel(planes, draws_ref, chol_ref, out_ref, near_ref, far_ref, repeat_ref, spread_ref, sums_ref, sems):
    walkers, steps, group = draws_ref.shape
    rows, orbitals = chol_ref.shape[1:]
    wide = orbitals // GROUPS
    depth = group * TILE
    parts = rows // TILE
    own_group = lax.axis_index("walk") * rows // wide
    upper = jnp.where(own_group >= GROUPS // 2, 1, 0)

    def columns(shift):
        return pl.ds(pl.multiple_of((own_group + shift) % GROUPS * wide, wide), wide)

    copies = []
    for step in range(steps):
        whole, half = pl.ds(step * group, group), pl.ds(step * group + upper * (group // 2), group // 2)
        pairs = [
            (chol_ref.at[whole, :, columns(0)], near_ref.at[step, :, :, pl.ds(0, wide)]),
            (chol_ref.at[whole, :, columns(1)], near_ref.at[step, :, :, pl.ds(wide, wide)]),
            (chol_ref.at[half, :, columns(2)], far_ref.at[step]),
        ]
        copies.append([pltpu.make_async_copy(*pair, sems.at[step, at]) for at, pair in enumerate(pairs)])
        for copy in copies[-1]:
            copy.start()

    owner = lax.broadcasted_iota(jnp.int32, (group, depth), 1) // TILE
    mine = owner == lax.broadcasted_iota(jnp.int32, (group, depth), 0)
    repeat_ref[...] = jnp.where(mine, 1.0, 0.0).astype(BF)
    lane_row = lax.broadcasted_iota(jnp.int32, (TILE, depth), 1) % TILE
    diagonal = lane_row == lax.broadcasted_iota(jnp.int32, (TILE, depth), 0)
    draws = draws_ref[...].astype(F32)

    def spread(step):
        repeated = jnp.dot(draws[:, step, :].astype(BF), repeat_ref[...], preferred_element_type=F32)
        for walker in range(walkers):
            block = jnp.where(diagonal, repeated[walker : walker + 1, :], 0.0)
            spread_ref[step % 2, walker * TILE : (walker + 1) * TILE, :] = block.astype(BF)

    def add(at, step, value):
        sums_ref[at] = value if step == 0 else sums_ref[at] + value

    spread(0)
    half_lanes = pl.ds(pl.multiple_of(upper * (depth // 2), depth // 2), depth // 2)
    for step in range(steps):
        if step + 1 < steps:
            spread(step + 1)
        for copy in copies[step]:
            copy.wait()
        far = []
        for part in range(parts):
            taken = slice(part * TILE, (part + 1) * TILE)
            right = near_ref[step, :, taken, :].reshape(depth, 2 * wide)
            add(part, step, jnp.dot(spread_ref[step % 2], right, preferred_element_type=F32))
            far.append(far_ref[step, :, taken, :].reshape(depth // 2, wide))
        right = jnp.concatenate(far, axis=1)
        add(parts, step, jnp.dot(spread_ref[step % 2, :, half_lanes], right, preferred_element_type=F32))

    for part in range(parts):
        for walker in range(walkers):
            place = (walker % planes) * (walkers // planes * parts) + walker // planes * parts + part
            taken = slice(walker * TILE, (walker + 1) * TILE)
            out_ref[place, :, : 2 * wide] = sums_ref[part, taken, :].astype(BF)
            out_ref[place, :, 2 * wide :] = sums_ref[parts, taken, part * wide : (part + 1) * wide].astype(BF)


def partial_operators(draws, chol_vectors, planes):
    walkers, steps, group = draws.shape
    vectors, rows, orbitals = chol_vectors.shape
    parts, wide = rows // TILE, orbitals // GROUPS
    vmem = pl.BlockSpec(memory_space=pltpu.VMEM)
    return pl.pallas_call(
        functools.partial(operator_kernel, planes),
        in_specs=[vmem, pl.BlockSpec(memory_space=pl.ANY)],
        out_specs=vmem,
        out_shape=jax.ShapeDtypeStruct((walkers * parts, TILE, 3 * wide), BF),
        scratch_shapes=[
            pltpu.VMEM((steps, group, rows, 2 * wide), BF),
            pltpu.VMEM((steps, group // 2, rows, wide), BF),
            pltpu.VMEM((group, group * TILE), BF),
            pltpu.VMEM((2, walkers * TILE, group * TILE), BF),
            pltpu.VMEM((parts + 1, walkers * TILE, 2 * wide), F32),
            pltpu.SemaphoreType.DMA((steps, 3)),
        ],
        compiler_params=pltpu.CompilerParams(vmem_limit_bytes=32 << 20),
        cost_estimate=pl.CostEstimate(
            flops=10 * walkers * TILE * vectors * rows * wide // 2,
            bytes_accessed=vectors * rows * wide * 5,
            transcendentals=0,
        ),
        name="operators",
    )(draws, in_hbm(chol_vectors))


def pieces_of(value, count):
    found = []
    for _ in range(count):
        piece = value.astype(BF)
        found.append(piece)
        value = value - piece.astype(F32)
    return found


def fine_dot(a, b):
    left = jnp.concatenate([a[0], a[0], a[1]], axis=1)
    right = jnp.concatenate([b[0], b[1], b[0]], axis=0)
    return jnp.dot(left, right, preferred_element_type=F32)


def full_dot(a, b):
    return jnp.dot(a, b, precision=lax.Precision.HIGHEST, preferred_element_type=F32)


def inverse_of(matrix):
    size = matrix.shape[0]
    shape = (size, size)
    one = jnp.where(lax.broadcasted_iota(jnp.int32, shape, 0) == lax.broadcasted_iota(jnp.int32, shape, 1), 1.0, 0.0)
    largest = jnp.max(jnp.sum(jnp.abs(matrix), axis=1, keepdims=True), axis=0, keepdims=True)
    guess = one * (1.5 / largest)
    halves = pieces_of(matrix, 2)

    def rough(carry):
        count, _, x = carry
        for _ in range(3):
            rest = one - fine_dot(halves, pieces_of(x, 2))
            x = x + fine_dot(pieces_of(x, 2), pieces_of(rest, 2))
        return count + 1, jnp.sum(rest * rest), x

    def exact(carry):
        count, _, x = carry
        rest = one - full_dot(matrix, x)
        return count + 1, jnp.sum(rest * rest), x + full_dot(x, rest)

    _, _, guess = lax.while_loop(
        lambda c: jnp.logical_and(c[0] < 14, c[1] > 1e-4), rough, (jnp.int32(0), jnp.float32(1), guess)
    )
    _, _, guess = lax.while_loop(
        lambda c: jnp.logical_and(c[0] < 6, c[1] > 1e-6), exact, (jnp.int32(0), jnp.float32(1), guess)
    )
    return guess


def solve_kernel(
    planes,
    own_rows_ref,
    other_rows_ref,
    own_walker_ref,
    other_walker_ref,
    own_ref,
    other_ref,
    propagated_ref,
    dual_ref,
    own_out_ref,
    other_out_ref,
    rows_ref,
    operators_ref,
    own_sem,
    other_sem,
):
    own_copy = pltpu.make_async_copy(own_ref, own_out_ref, own_sem)
    other_copy = pltpu.make_async_copy(other_ref, other_out_ref, other_sem)
    own_copy.start()
    other_copy.start()
    core, chol = lax.axis_index("walk") % 2, lax.axis_index("chol")
    slabs, wide = own_rows_ref.shape[0] // planes, own_rows_ref.shape[2] // 3
    for slab in range(slabs):
        for from_ref, side in ((own_rows_ref, core), (other_rows_ref, 1 - core)):
            summed = from_ref[slab].astype(F32)
            for plane in range(1, planes):
                summed = summed + from_ref[plane * slabs + slab].astype(F32)
            rows_ref[pl.ds(pl.multiple_of((2 * slab + side) * TILE, TILE), TILE), :] = summed
    group = lambda k: slice(k % GROUPS * wide, (k % GROUPS + 1) * wide)
    for k in range(GROUPS):
        operators_ref[group(k), group(k)] = rows_ref[group(k), group(0)].astype(BF)
        after = rows_ref[group(k), group(1)]
        operators_ref[group(k), group(k + 1)] = after.astype(BF)
        operators_ref[group(k + 1), group(k)] = after.T.astype(BF)
    for k in range(GROUPS // 2):
        one, two = rows_ref[group(k), group(2)], rows_ref[group(k + 2), group(2)]
        operators_ref[group(k), group(k + 2)] = (one + two.T).astype(BF)
        operators_ref[group(k + 2), group(k)] = (one.T + two).astype(BF)
    mine = jnp.where(core == chol, 1.0, 0.0)
    walker = own_walker_ref[...].astype(F32) * mine + other_walker_ref[...].astype(F32) * (1.0 - mine)
    taylor_term = walker.astype(BF)
    transposed = taylor_term.T
    propagated = walker
    for degree in range(1, TERMS + 1):
        applied = jnp.dot(operators_ref[...], taylor_term, preferred_element_type=F32)
        taylor_term = (applied / degree).astype(BF)
        propagated = propagated + taylor_term.astype(F32)
    propagated_ref[...] = propagated
    correlation = None
    for piece in pieces_of(propagated, 3):
        part = jnp.dot(transposed, piece, preferred_element_type=F32)
        correlation = part if correlation is None else correlation + part
    dual_ref[...] = full_dot(propagated, inverse_of(correlation)).astype(BF)
    own_copy.wait()
    other_copy.wait()


def solve(own_rows, other_rows, own_walker, other_walker, own, other, planes):
    orbitals = own_walker.shape[0]
    vmem, anywhere = pl.BlockSpec(memory_space=pltpu.VMEM), pl.BlockSpec(memory_space=pl.ANY)
    return pl.pallas_call(
        functools.partial(solve_kernel, planes),
        in_specs=[vmem] * 4 + [anywhere] * 2,
        out_specs=[vmem] * 4,
        out_shape=[
            jax.ShapeDtypeStruct(own_walker.shape, F32),
            jax.ShapeDtypeStruct(own_walker.shape, BF),
            pltpu.VMEM(own.shape, BF),
            pltpu.VMEM(other.shape, BF),
        ],
        scratch_shapes=[
            pltpu.VMEM((orbitals, own_rows.shape[2]), F32),
            pltpu.VMEM((orbitals, orbitals), BF),
            pltpu.SemaphoreType.DMA,
            pltpu.SemaphoreType.DMA,
        ],
        compiler_params=pltpu.CompilerParams(vmem_limit_bytes=16 << 20),
        cost_estimate=pl.CostEstimate(flops=6 * 10**9, bytes_accessed=16 << 20, transcendentals=0),
        name="solve",
    )(own_rows, other_rows, own_walker, other_walker, in_hbm(own), in_hbm(other))


def energy_kernel(group, sub, own_ref, other_ref, *refs):
    dual_refs, out_ref = refs[:-1], refs[-1]
    vectors, occ, orbitals = own_ref.shape
    pairs = [jnp.concatenate([ref[0], ref[1]], axis=1) for ref in dual_refs]
    count = 2 * len(pairs)
    out_ref[...] = jnp.zeros_like(out_ref)
    for vectors_ref in (own_ref, other_ref):

        @pl.loop(0, vectors, step=group)
        def _(start):
            totals = [None] * count
            for at in range(0, group, sub):
                left = vectors_ref[pl.ds(start + at, sub)].reshape(sub * occ, orbitals)
                for pair, right in enumerate(pairs):
                    products = jnp.dot(left, right, preferred_element_type=F32)
                    for member in range(2):
                        for vector in range(sub):
                            block = products[vector * occ : (vector + 1) * occ, member * occ : (member + 1) * occ]
                            term = (block * block.T).reshape(occ // 8, 8, occ).sum(0)
                            slot = 2 * pair + member
                            totals[slot] = term if totals[slot] is None else totals[slot] + term
            for slot in range(count):
                out_ref[slot] += totals[slot]


def energies(own, other, duals, group=64, sub=2):
    vectors, occ, orbitals = own.shape
    count = 2 * len(duals)
    vmem = pl.BlockSpec(memory_space=pltpu.VMEM)
    return pl.pallas_call(
        functools.partial(energy_kernel, group, sub),
        in_specs=[vmem] * (2 + len(duals)),
        out_specs=vmem,
        out_shape=jax.ShapeDtypeStruct((count, 8, occ), F32),
        compiler_params=pltpu.CompilerParams(vmem_limit_bytes=16 << 20),
        cost_estimate=pl.CostEstimate(
            flops=4 * vectors * count * occ * occ * orbitals,
            bytes_accessed=4 * vectors * occ * orbitals,
            transcendentals=0,
        ),
        name="energies",
    )(in_vmem(own), in_vmem(other), *duals)


def flat(chol, z, y, core, walk):
    return chol * walk + (z * 2 + y) * 2 + core


def per_device(field_draws, chol_vectors, rotated_vectors, walkers):
    planes, walk = lax.axis_size("chol"), lax.axis_size("walk")
    depth = walk // 4
    chol, place = lax.axis_index("chol"), lax.axis_index("walk")
    core, z = place % 2, place // 4
    slab_vectors, slab_rows, orbitals = chol_vectors.shape
    occ = walkers.shape[2]
    swap = [(i, i ^ 1) for i in range(walk)]
    every = [(c, zz, y, k) for c in range(2) for zz in range(depth) for y in range(2) for k in range(2)]

    def send(array, target):
        pairs = [(flat(*at, walk), flat(*target(*at), walk)) for at in every if target(*at) is not None]
        return lax.ppermute(array, BOTH, pairs)

    other_vectors = lax.ppermute(rotated_vectors, "walk", swap)
    other_walker = lax.ppermute(walkers, "walk", swap)

    lanes = walkers.shape[2]
    spread = jnp.broadcast_to(field_draws.reshape(1, slab_vectors // lanes, lanes), (walk, slab_vectors // lanes, lanes))
    draws = lax.all_to_all(spread, "walk", split_axis=0, concat_axis=0, tiled=True)
    partial = partial_operators(draws, chol_vectors, planes)
    rows = lax.all_to_all(partial, BOTH, split_axis=0, concat_axis=0, tiled=True)
    other_rows = lax.ppermute(rows, "walk", swap)

    propagated, dual, own, other = solve(
        rows, other_rows, walkers[0], other_walker[0], rotated_vectors, other_vectors, planes
    )

    def first(c, zz, y, k):
        return (c, zz ^ 1 if zz // 2 == k else zz ^ 2, y, zz // 2)

    def second(c, zz, y, k):
        return (c, zz ^ 3, y, k) if zz // 2 == k else None

    turn = lambda c, zz, y, k: (c, zz, 1 - y, k) if k == 0 else (1 - c, zz, y, k)
    back = lambda c, zz, y, k: (1 - c, zz, y, k) if k == 0 else (c, zz, 1 - y, k)
    near, far = send(dual, first), send(dual, second)
    odd, inside = z % 2 == 1, z // 2 == core
    pick = lambda here, low, high: jnp.where(inside, jnp.where(here, dual, near), jnp.where(low, near, far))
    mine = jnp.stack([pick(~odd, ~odd, odd), pick(odd, odd, ~odd)])
    across = send(propagated, lambda c, zz, y, k: (1 - c, zz, y, k) if k == c else None)
    one = send(mine, turn)
    terms = [energies(own, other, [mine])]
    one, mine, terms[0] = lax.optimization_barrier((one, mine, terms[0]))
    over = send(mine, back)
    terms.append(energies(own, other, [one]))
    one, over, terms[1] = lax.optimization_barrier((one, over, terms[1]))
    both = send(one, back)
    terms.append(energies(own, other, [over]))
    both, terms[2] = lax.optimization_barrier((both, terms[2]))
    terms.append(energies(own, other, [both]))
    terms = jnp.concatenate(terms, 0).sum(1)

    y = place // 2 % 2
    slots = []
    for order in range(4):
        first_axis, second_axis = order % 2, order // 2
        y_flip = jnp.where(core == 0, first_axis, second_axis)
        x_flip = jnp.where(core == 0, second_axis, first_axis)
        for parity in range(2):
            slots.append(((2 * core + parity) * 2 + (y ^ y_flip)) * 2 + (chol ^ x_flip))
    slots = jnp.stack(slots)
    hit = (slots[None, :, None] == jnp.arange(walk)[:, None, None]).astype(F32)
    sent = (hit * terms[None]).sum(1)
    sent = jnp.broadcast_to(sent, (planes,) + sent.shape).reshape(planes * walk, occ)
    came = lax.all_to_all(sent, BOTH, split_axis=0, concat_axis=0, tiled=True)
    propagated = jnp.where(core == chol, propagated, across)[None]
    return propagated, -0.5 * came.sum().reshape(1)


def per_device_plain(field_draws, chol_vectors, rotated_vectors, walkers):
    local_walkers, orbitals, occ = walkers.shape
    total_walkers = local_walkers * lax.axis_size("walk")
    slab_vectors, slab_rows, _ = chol_vectors.shape
    all_draws = lax.all_gather(field_draws, "walk", axis=0, tiled=True)
    partial_rows = jnp.dot(
        all_draws, chol_vectors.reshape(slab_vectors, slab_rows * orbitals), preferred_element_type=F32
    )
    partial_rows = partial_rows.reshape(total_walkers, slab_rows, orbitals)
    summed_rows = lax.psum(partial_rows, "chol").astype(BF)
    operators = lax.all_to_all(summed_rows, "walk", split_axis=0, concat_axis=1, tiled=True)
    propagated = jax.vmap(propagate)(operators, walkers)
    duals = jax.vmap(dual_of)(walkers, propagated)
    dual_cols = jnp.transpose(duals, (1, 0, 2)).reshape(orbitals, local_walkers * occ)
    columns = lax.all_gather(dual_cols, "walk", axis=1, tiled=True)

    def vector_step(vector, summed):
        single = lax.dynamic_index_in_dim(rotated_vectors, vector, 0, keepdims=False)
        tiled = jnp.dot(single, columns, preferred_element_type=F32).reshape(occ, total_walkers, occ)
        return summed + jnp.einsum("iwj,jwi->w", tiled, tiled)

    totals = lax.fori_loop(0, rotated_vectors.shape[0], vector_step, jnp.zeros((total_walkers,), F32))
    summed = lax.psum(totals, BOTH)
    mine = lax.dynamic_slice_in_dim(summed, lax.axis_index("walk") * local_walkers, local_walkers, 0)
    return propagated, -0.5 * mine


def solution(mesh):
    planes, walk = mesh.shape["chol"], mesh.shape["walk"]

    def step(field_draws, chol_vectors, rotated_vectors, walkers):
        rows, orbitals = chol_vectors.shape[1:]
        occ = walkers.shape[2]
        fits = planes == 2 and walk == 16 and walkers.shape[0] == 1 and rows == 2 * TILE and orbitals == GROUPS * occ
        body = per_device if fits else per_device_plain
        return body(field_draws, chol_vectors, rotated_vectors, walkers)

    return jax.shard_map(
        step,
        mesh=mesh,
        in_specs=(
            P("walk", "chol"),
            P("chol", "walk", None),
            P(("chol", "walk"), None, None),
            P("walk", None, None),
        ),
        out_specs=(P("walk", None, None), P("walk")),
        check_vma=False,
    )
```

```python
import functools

import jax
import jax.numpy as jnp
from jax import lax
from jax.experimental import pallas as pl
from jax.experimental.pallas import tpu as pltpu
from jax.sharding import PartitionSpec as P

TERMS = 4
TILE = 16
GROUPS = 4
PRELOADED = 1
BF = jnp.bfloat16
F32 = jnp.float32
BOTH = ("chol", "walk")


def in_hbm(array):
    return pltpu.with_memory_space_constraint(array, pltpu.HBM)


def in_vmem(array):
    return pltpu.with_memory_space_constraint(array, pltpu.VMEM)


def solve_dual(correlation, transposed):
    gram = jnp.dot(correlation, correlation.T, precision=lax.Precision.HIGHEST)
    factor = jnp.linalg.cholesky(gram)
    right = jnp.dot(correlation, transposed, precision=lax.Precision.HIGHEST)
    return jax.scipy.linalg.cho_solve((factor, True), right)


def propagate(operators, walkers):
    taylor_term = walkers
    propagated = walkers.astype(F32)
    for degree in range(1, TERMS + 1):
        applied = jnp.dot(operators, taylor_term, preferred_element_type=F32)
        taylor_term = (applied / degree).astype(BF)
        propagated = propagated + taylor_term.astype(F32)
    return propagated


def dual_of(walkers, propagated):
    correlation = jnp.dot(walkers.astype(F32).T, propagated, precision=lax.Precision.HIGHEST)
    return solve_dual(correlation, propagated.T).T.astype(BF)


def column_copies(chol_ref, near_refs, far_refs, sems, first, group):
    rows, orbitals = chol_ref.shape[1:]
    wide = orbitals // GROUPS
    own_group = lax.axis_index("walk") * rows // wide
    upper = jnp.where(own_group >= GROUPS // 2, 1, 0)

    def columns(shift):
        return pl.ds(pl.multiple_of((own_group + shift) % GROUPS * wide, wide), wide)

    copies = []
    for at, (near_ref, far_ref) in enumerate(zip(near_refs, far_refs)):
        start = (first + at) * group
        whole, half = pl.ds(start, group), pl.ds(start + upper * (group // 2), group // 2)
        pairs = [
            (chol_ref.at[whole, :, columns(0)], near_ref.at[:, :, pl.ds(0, wide)]),
            (chol_ref.at[whole, :, columns(1)], near_ref.at[:, :, pl.ds(wide, wide)]),
            (chol_ref.at[half, :, columns(2)], far_ref),
        ]
        copies.append([pltpu.make_async_copy(*pair, sems.at[at, nth]) for nth, pair in enumerate(pairs)])
    return copies, upper


def preload_kernel(group, chol_ref, *refs):
    steps = len(refs) // 2
    copies, _ = column_copies(chol_ref, refs[:steps], refs[steps:-1], refs[-1], 0, group)
    for step in copies:
        for copy in step:
            copy.start()
    for step in copies:
        for copy in step:
            copy.wait()


def preload(chol_vectors, steps, group):
    _, rows, orbitals = chol_vectors.shape
    wide = orbitals // GROUPS
    return pl.pallas_call(
        functools.partial(preload_kernel, group),
        in_specs=[pl.BlockSpec(memory_space=pl.ANY)],
        out_specs=[pl.BlockSpec(memory_space=pltpu.VMEM)] * (2 * steps),
        out_shape=[pltpu.VMEM((group, rows, 2 * wide), BF)] * steps
        + [pltpu.VMEM((group // 2, rows, wide), BF)] * steps,
        scratch_shapes=[pltpu.SemaphoreType.DMA((steps, 3))],
        compiler_params=pltpu.CompilerParams(vmem_limit_bytes=1 << 20),
        cost_estimate=pl.CostEstimate(
            flops=0, bytes_accessed=10 * steps * group * rows * wide, transcendentals=0
        ),
        name="preload",
    )(in_hbm(chol_vectors))


def operator_kernel(planes, loaded, draws_ref, *refs):
    near_refs, far_refs = list(refs[:loaded]), list(refs[loaded : 2 * loaded])
    chol_ref, out_ref, near_ref, far_ref, repeat_ref, spread_ref, sums_ref, sems = refs[2 * loaded :]
    walkers, steps, group = draws_ref.shape
    rows, orbitals = chol_ref.shape[1:]
    wide = orbitals // GROUPS
    depth = group * TILE
    parts = rows // TILE
    rest = [near_ref.at[at] for at in range(steps - loaded)], [far_ref.at[at] for at in range(steps - loaded)]
    near_refs, far_refs = near_refs + rest[0], far_refs + rest[1]
    copies, upper = column_copies(chol_ref, *rest, sems, loaded, group)
    for step in copies:
        for copy in step:
            copy.start()

    owner = lax.broadcasted_iota(jnp.int32, (group, depth), 1) // TILE
    mine = owner == lax.broadcasted_iota(jnp.int32, (group, depth), 0)
    repeat_ref[...] = jnp.where(mine, 1.0, 0.0).astype(BF)
    lane_row = lax.broadcasted_iota(jnp.int32, (TILE, depth), 1) % TILE
    diagonal = lane_row == lax.broadcasted_iota(jnp.int32, (TILE, depth), 0)
    draws = draws_ref[...].astype(F32)

    def spread(step):
        repeated = jnp.dot(draws[:, step, :].astype(BF), repeat_ref[...], preferred_element_type=F32)
        for walker in range(walkers):
            block = jnp.where(diagonal, repeated[walker : walker + 1, :], 0.0)
            spread_ref[step % 2, walker * TILE : (walker + 1) * TILE, :] = block.astype(BF)

    def add(at, step, value):
        sums_ref[at] = value if step == 0 else sums_ref[at] + value

    spread(0)
    half_lanes = pl.ds(pl.multiple_of(upper * (depth // 2), depth // 2), depth // 2)
    for step in range(steps):
        if step + 1 < steps:
            spread(step + 1)
        near, far_at = near_refs[step], far_refs[step]
        if step >= loaded:
            for copy in copies[step - loaded]:
                copy.wait()
        far = []
        for part in range(parts):
            taken = slice(part * TILE, (part + 1) * TILE)
            right = near[:, taken, :].reshape(depth, 2 * wide)
            add(part, step, jnp.dot(spread_ref[step % 2], right, preferred_element_type=F32))
            far.append(far_at[:, taken, :].reshape(depth // 2, wide))
        right = jnp.concatenate(far, axis=1)
        add(parts, step, jnp.dot(spread_ref[step % 2, :, half_lanes], right, preferred_element_type=F32))

    for part in range(parts):
        for walker in range(walkers):
            place = (walker % planes) * (walkers // planes * parts) + walker // planes * parts + part
            taken = slice(walker * TILE, (walker + 1) * TILE)
            out_ref[place, :, : 2 * wide] = sums_ref[part, taken, :].astype(BF)
            out_ref[place, :, 2 * wide :] = sums_ref[parts, taken, part * wide : (part + 1) * wide].astype(BF)


def partial_operators(draws, chol_vectors, held, planes):
    walkers, steps, group = draws.shape
    vectors, rows, orbitals = chol_vectors.shape
    parts, wide = rows // TILE, orbitals // GROUPS
    loaded = len(held) // 2
    rest = steps - loaded
    vmem = pl.BlockSpec(memory_space=pltpu.VMEM)
    return pl.pallas_call(
        functools.partial(operator_kernel, planes, loaded),
        in_specs=[vmem] * (1 + len(held)) + [pl.BlockSpec(memory_space=pl.ANY)],
        out_specs=vmem,
        out_shape=jax.ShapeDtypeStruct((walkers * parts, TILE, 3 * wide), BF),
        scratch_shapes=[
            pltpu.VMEM((rest, group, rows, 2 * wide), BF),
            pltpu.VMEM((rest, group // 2, rows, wide), BF),
            pltpu.VMEM((group, group * TILE), BF),
            pltpu.VMEM((2, walkers * TILE, group * TILE), BF),
            pltpu.VMEM((parts + 1, walkers * TILE, 2 * wide), F32),
            pltpu.SemaphoreType.DMA((rest, 3)),
        ],
        compiler_params=pltpu.CompilerParams(vmem_limit_bytes=24 << 20),
        cost_estimate=pl.CostEstimate(
            flops=10 * walkers * TILE * vectors * rows * wide // 2,
            bytes_accessed=vectors * rows * wide * 5,
            transcendentals=0,
        ),
        name="operators",
    )(draws, *[in_vmem(part) for part in held], in_hbm(chol_vectors))


def pieces_of(value, count):
    found = []
    for _ in range(count):
        piece = value.astype(BF)
        found.append(piece)
        value = value - piece.astype(F32)
    return found


def fine_dot(a, b):
    left = jnp.concatenate([a[0], a[0], a[1]], axis=1)
    right = jnp.concatenate([b[0], b[1], b[0]], axis=0)
    return jnp.dot(left, right, preferred_element_type=F32)


def full_dot(a, b):
    return jnp.dot(a, b, precision=lax.Precision.HIGHEST, preferred_element_type=F32)


def inverse_of(matrix):
    size = matrix.shape[0]
    shape = (size, size)
    one = jnp.where(lax.broadcasted_iota(jnp.int32, shape, 0) == lax.broadcasted_iota(jnp.int32, shape, 1), 1.0, 0.0)
    largest = jnp.max(jnp.sum(jnp.abs(matrix), axis=1, keepdims=True), axis=0, keepdims=True)
    scale = 1.5 / largest
    guess = scale * (2.0 * one - scale * matrix)
    halves = pieces_of(matrix, 2)

    def rough(carry):
        count, _, x = carry
        for _ in range(4):
            rest = one - fine_dot(halves, pieces_of(x, 2))
            x = x + fine_dot(pieces_of(x, 2), pieces_of(rest, 2))
        return count + 1, jnp.sum(rest * rest), x

    def exact(carry):
        count, _, x = carry
        rest = one - full_dot(matrix, x)
        return count + 1, jnp.sum(rest * rest), x + full_dot(x, rest)

    _, _, guess = lax.while_loop(
        lambda c: jnp.logical_and(c[0] < 10, c[1] > 1e-4), rough, (jnp.int32(0), jnp.float32(1), guess)
    )
    _, _, guess = lax.while_loop(
        lambda c: jnp.logical_and(c[0] < 6, c[1] > 1e-6), exact, (jnp.int32(0), jnp.float32(1), guess)
    )
    return guess


def solve_kernel(
    planes,
    own_rows_ref,
    other_rows_ref,
    own_walker_ref,
    other_walker_ref,
    own_ref,
    other_ref,
    propagated_ref,
    dual_ref,
    own_out_ref,
    other_out_ref,
    rows_ref,
    operators_ref,
    own_sem,
    other_sem,
):
    own_copy = pltpu.make_async_copy(own_ref, own_out_ref, own_sem)
    other_copy = pltpu.make_async_copy(other_ref, other_out_ref, other_sem)
    own_copy.start()
    other_copy.start()
    core, chol = lax.axis_index("walk") % 2, lax.axis_index("chol")
    slabs, wide = own_rows_ref.shape[0] // planes, own_rows_ref.shape[2] // 3
    for slab in range(slabs):
        for from_ref, side in ((own_rows_ref, core), (other_rows_ref, 1 - core)):
            summed = from_ref[slab].astype(F32)
            for plane in range(1, planes):
                summed = summed + from_ref[plane * slabs + slab].astype(F32)
            rows_ref[pl.ds(pl.multiple_of((2 * slab + side) * TILE, TILE), TILE), :] = summed
    group = lambda k: slice(k % GROUPS * wide, (k % GROUPS + 1) * wide)
    for k in range(GROUPS):
        operators_ref[group(k), group(k)] = rows_ref[group(k), group(0)].astype(BF)
        after = rows_ref[group(k), group(1)]
        operators_ref[group(k), group(k + 1)] = after.astype(BF)
        operators_ref[group(k + 1), group(k)] = after.T.astype(BF)
    for k in range(GROUPS // 2):
        one, two = rows_ref[group(k), group(2)], rows_ref[group(k + 2), group(2)]
        operators_ref[group(k), group(k + 2)] = (one + two.T).astype(BF)
        operators_ref[group(k + 2), group(k)] = (one.T + two).astype(BF)
    mine = jnp.where(core == chol, 1.0, 0.0)
    walker = own_walker_ref[...].astype(F32) * mine + other_walker_ref[...].astype(F32) * (1.0 - mine)
    taylor_term = walker.astype(BF)
    transposed = taylor_term.T
    propagated = walker
    for degree in range(1, TERMS + 1):
        applied = jnp.dot(operators_ref[...], taylor_term, preferred_element_type=F32)
        taylor_term = (applied / degree).astype(BF)
        propagated = propagated + taylor_term.astype(F32)
    propagated_ref[...] = propagated
    correlation = None
    for piece in pieces_of(propagated, 3):
        part = jnp.dot(transposed, piece, preferred_element_type=F32)
        correlation = part if correlation is None else correlation + part
    dual_ref[...] = full_dot(propagated, inverse_of(correlation)).astype(BF)
    own_copy.wait()
    other_copy.wait()


def solve(own_rows, other_rows, own_walker, other_walker, own, other, planes):
    orbitals = own_walker.shape[0]
    vmem, anywhere = pl.BlockSpec(memory_space=pltpu.VMEM), pl.BlockSpec(memory_space=pl.ANY)
    return pl.pallas_call(
        functools.partial(solve_kernel, planes),
        in_specs=[vmem] * 4 + [anywhere] * 2,
        out_specs=[vmem] * 4,
        out_shape=[
            jax.ShapeDtypeStruct(own_walker.shape, F32),
            jax.ShapeDtypeStruct(own_walker.shape, BF),
            pltpu.VMEM(own.shape, BF),
            pltpu.VMEM(other.shape, BF),
        ],
        scratch_shapes=[
            pltpu.VMEM((orbitals, own_rows.shape[2]), F32),
            pltpu.VMEM((orbitals, orbitals), BF),
            pltpu.SemaphoreType.DMA,
            pltpu.SemaphoreType.DMA,
        ],
        compiler_params=pltpu.CompilerParams(vmem_limit_bytes=16 << 20),
        cost_estimate=pl.CostEstimate(flops=6 * 10**9, bytes_accessed=16 << 20, transcendentals=0),
        name="solve",
    )(own_rows, other_rows, own_walker, other_walker, in_hbm(own), in_hbm(other))


def energy_kernel(group, sub, own_ref, other_ref, *refs):
    dual_refs, out_ref = refs[:-1], refs[-1]
    vectors, occ, orbitals = own_ref.shape
    pairs = [jnp.concatenate([ref[0], ref[1]], axis=1) for ref in dual_refs]
    count = 2 * len(pairs)
    out_ref[...] = jnp.zeros_like(out_ref)
    for vectors_ref in (own_ref, other_ref):

        @pl.loop(0, vectors, step=group)
        def _(start):
            totals = [None] * count
            for at in range(0, group, sub):
                left = vectors_ref[pl.ds(start + at, sub)].reshape(sub * occ, orbitals)
                for pair, right in enumerate(pairs):
                    products = jnp.dot(left, right, preferred_element_type=F32)
                    for member in range(2):
                        for vector in range(sub):
                            block = products[vector * occ : (vector + 1) * occ, member * occ : (member + 1) * occ]
                            term = (block * block.T).reshape(occ // 8, 8, occ).sum(0)
                            slot = 2 * pair + member
                            totals[slot] = term if totals[slot] is None else totals[slot] + term
            for slot in range(count):
                out_ref[slot] += totals[slot]


def energies(own, other, duals, group=64, sub=2):
    vectors, occ, orbitals = own.shape
    count = 2 * len(duals)
    vmem = pl.BlockSpec(memory_space=pltpu.VMEM)
    return pl.pallas_call(
        functools.partial(energy_kernel, group, sub),
        in_specs=[vmem] * (2 + len(duals)),
        out_specs=vmem,
        out_shape=jax.ShapeDtypeStruct((count, 8, occ), F32),
        compiler_params=pltpu.CompilerParams(vmem_limit_bytes=16 << 20),
        cost_estimate=pl.CostEstimate(
            flops=4 * vectors * count * occ * occ * orbitals,
            bytes_accessed=4 * vectors * occ * orbitals,
            transcendentals=0,
        ),
        name="energies",
    )(in_vmem(own), in_vmem(other), *duals)


def flat(chol, z, y, core, walk):
    return chol * walk + (z * 2 + y) * 2 + core


def per_device(field_draws, chol_vectors, rotated_vectors, walkers):
    planes, walk = lax.axis_size("chol"), lax.axis_size("walk")
    depth = walk // 4
    chol, place = lax.axis_index("chol"), lax.axis_index("walk")
    core, z = place % 2, place // 4
    slab_vectors, slab_rows, orbitals = chol_vectors.shape
    occ = walkers.shape[2]
    swap = [(i, i ^ 1) for i in range(walk)]
    every = [(c, zz, y, k) for c in range(2) for zz in range(depth) for y in range(2) for k in range(2)]

    def send(array, target):
        pairs = [(flat(*at, walk), flat(*target(*at), walk)) for at in every if target(*at) is not None]
        return lax.ppermute(array, BOTH, pairs)

    other_vectors = lax.ppermute(rotated_vectors, "walk", swap)
    other_walker = lax.ppermute(walkers, "walk", swap)

    lanes = walkers.shape[2]
    spread = jnp.broadcast_to(field_draws.reshape(1, slab_vectors // lanes, lanes), (walk, slab_vectors // lanes, lanes))
    draws = lax.all_to_all(spread, "walk", split_axis=0, concat_axis=0, tiled=True)
    held = preload(chol_vectors, PRELOADED, lanes)
    partial = partial_operators(draws, chol_vectors, held, planes)
    rows = lax.all_to_all(partial, BOTH, split_axis=0, concat_axis=0, tiled=True)
    other_rows = lax.ppermute(rows, "walk", swap)

    propagated, dual, own, other = solve(
        rows, other_rows, walkers[0], other_walker[0], rotated_vectors, other_vectors, planes
    )

    def first(c, zz, y, k):
        return (c, zz ^ 1 if zz // 2 == k else zz ^ 2, y, zz // 2)

    def second(c, zz, y, k):
        return (c, zz ^ 3, y, k) if zz // 2 == k else None

    turn = lambda c, zz, y, k: (c, zz, 1 - y, k) if k == 0 else (1 - c, zz, y, k)
    back = lambda c, zz, y, k: (1 - c, zz, y, k) if k == 0 else (c, zz, 1 - y, k)
    near, far = send(dual, first), send(dual, second)
    odd, inside = z % 2 == 1, z // 2 == core
    pick = lambda here, low, high: jnp.where(inside, jnp.where(here, dual, near), jnp.where(low, near, far))
    mine = jnp.stack([pick(~odd, ~odd, odd), pick(odd, odd, ~odd)])
    across = send(propagated, lambda c, zz, y, k: (1 - c, zz, y, k) if k == c else None)
    one = send(mine, turn)
    terms = [energies(own, other, [mine])]
    one, mine, terms[0] = lax.optimization_barrier((one, mine, terms[0]))
    over = send(mine, back)
    terms.append(energies(own, other, [one]))
    one, over, terms[1] = lax.optimization_barrier((one, over, terms[1]))
    both = send(one, back)
    terms.append(energies(own, other, [over]))
    both, terms[2] = lax.optimization_barrier((both, terms[2]))
    terms.append(energies(own, other, [both]))
    terms = jnp.concatenate(terms, 0).sum(1)

    y = place // 2 % 2
    slots = []
    for order in range(4):
        first_axis, second_axis = order % 2, order // 2
        y_flip = jnp.where(core == 0, first_axis, second_axis)
        x_flip = jnp.where(core == 0, second_axis, first_axis)
        for parity in range(2):
            slots.append(((2 * core + parity) * 2 + (y ^ y_flip)) * 2 + (chol ^ x_flip))
    slots = jnp.stack(slots)
    hit = (slots[None, :, None] == jnp.arange(walk)[:, None, None]).astype(F32)
    sent = (hit * terms[None]).sum(1)
    sent = jnp.broadcast_to(sent, (planes,) + sent.shape).reshape(planes * walk, occ)
    came = lax.all_to_all(sent, BOTH, split_axis=0, concat_axis=0, tiled=True)
    propagated = jnp.where(core == chol, propagated, across)[None]
    return propagated, -0.5 * came.sum().reshape(1)


def per_device_plain(field_draws, chol_vectors, rotated_vectors, walkers):
    local_walkers, orbitals, occ = walkers.shape
    total_walkers = local_walkers * lax.axis_size("walk")
    slab_vectors, slab_rows, _ = chol_vectors.shape
    all_draws = lax.all_gather(field_draws, "walk", axis=0, tiled=True)
    partial_rows = jnp.dot(
        all_draws, chol_vectors.reshape(slab_vectors, slab_rows * orbitals), preferred_element_type=F32
    )
    partial_rows = partial_rows.reshape(total_walkers, slab_rows, orbitals)
    summed_rows = lax.psum(partial_rows, "chol").astype(BF)
    operators = lax.all_to_all(summed_rows, "walk", split_axis=0, concat_axis=1, tiled=True)
    propagated = jax.vmap(propagate)(operators, walkers)
    duals = jax.vmap(dual_of)(walkers, propagated)
    dual_cols = jnp.transpose(duals, (1, 0, 2)).reshape(orbitals, local_walkers * occ)
    columns = lax.all_gather(dual_cols, "walk", axis=1, tiled=True)

    def vector_step(vector, summed):
        single = lax.dynamic_index_in_dim(rotated_vectors, vector, 0, keepdims=False)
        tiled = jnp.dot(single, columns, preferred_element_type=F32).reshape(occ, total_walkers, occ)
        return summed + jnp.einsum("iwj,jwi->w", tiled, tiled)

    totals = lax.fori_loop(0, rotated_vectors.shape[0], vector_step, jnp.zeros((total_walkers,), F32))
    summed = lax.psum(totals, BOTH)
    mine = lax.dynamic_slice_in_dim(summed, lax.axis_index("walk") * local_walkers, local_walkers, 0)
    return propagated, -0.5 * mine


def solution(mesh):
    planes, walk = mesh.shape["chol"], mesh.shape["walk"]

    def step(field_draws, chol_vectors, rotated_vectors, walkers):
        rows, orbitals = chol_vectors.shape[1:]
        occ = walkers.shape[2]
        fits = planes == 2 and walk == 16 and walkers.shape[0] == 1 and rows == 2 * TILE and orbitals == GROUPS * occ
        body = per_device if fits else per_device_plain
        return body(field_draws, chol_vectors, rotated_vectors, walkers)

    return jax.shard_map(
        step,
        mesh=mesh,
        in_specs=(
            P("walk", "chol"),
            P("chol", "walk", None),
            P(("chol", "walk"), None, None),
            P("walk", None, None),
        ),
        out_specs=(P("walk", None, None), P("walk")),
        check_vma=False,
    )
```
